32 devices in a mesh: grp: 2 (over x), dom: 16 (over z, y, core).
Axes of the slice: x: 2, y: 2, z: 4, core: 2. Of those that a mesh axis runs over, the one named last changes fastest.
Arguments:
- features: bfloat16 [24576, 128], P(('grp', 'dom')), parts along dimension 0, may hold values from -6 to 6
- block_tiles: bfloat16 [192, 128, 44, 128], P(('grp', 'dom')), parts along dimension 0, may hold values from -0.078125 to 0.078125
- block_cols: int32 [192, 44], P(('grp', 'dom')), parts along dimension 0, may hold values from 0 to 21, as said below
- halo_request: int32 [32, 16], P(('grp', 'dom')), parts along dimension 0, may hold values from 0 to 5
- labels: int32 [24576], P(('grp', 'dom')), parts along dimension 0, may hold values from 0 to 171
- weight_one: bfloat16 [128, 256], replicated, may hold values from -0.5 to 0.5
- weight_two: bfloat16 [256, 172], replicated, may hold values from -0.375 to 0.375
Outputs:
- logits: float32 [24576, 172], P(('grp', 'dom')), parts along dimension 0
- grad_one: float32 [256, 256], P('grp'), parts along dimension 0
- grad_two: float32 [512, 172], P('grp'), parts along dimension 0
The draws below stay inside these ranges and needn't reach their ends.
There are 2 independent parts, one for each index of `grp`. The reference program is written for one: setup_inputs(seed, part) draws one part's arguments, and reference() takes and returns one part's arrays. A program takes and returns all parts, laid end to end along the dimension named above; an argument that names none is the same for every part. Nothing has to cross between parts.
Inputs may be any that keep to these rules, and one draw needn't show every extreme that they name: `block_cols`: among the 264 entries of each partition's block rows, every table entry 0 to 21 appears.
All inputs are finite; a program needn't handle non-finite values.
Results may differ from the reference program's by a relative error of at most 0.0039.
The reference program's roundings to bfloat16 on the way count: a program that leaves them out, or rounds other values in their place, can miss the bound.
Values may be sent and summed in bfloat16 or wider, within the bound.
A program may use at most 128 MiB of HBM per device.

```python
import jax
import jax.numpy as jnp
from jax import lax

F = 128
H = 256
C = 172
BS = 128
KR = 44
NB_DEV = 6
NPART = 16
NBLOCKS = 96
NODES = 12288


def draw_block_cols(key, part):
    key = jax.random.fold_in(key, 7)
    keys = jax.random.split(key, NPART)
    table_size = NB_DEV + NPART
    extra_count = NB_DEV * KR - table_size

    def one_partition(sub):
        first, second, third, fourth, fifth = jax.random.split(sub, 5)
        every = jax.random.permutation(first, table_size).astype(jnp.int32)
        remote = jax.random.randint(second, (extra_count,), 0, table_size).astype(jnp.int32)
        local = jax.random.randint(fourth, (extra_count,), 0, NB_DEV).astype(jnp.int32)
        pick = jax.random.randint(fifth, (extra_count,), 0, 4)
        extra = jnp.where(pick < 3, local, remote).astype(jnp.int32)
        joined = jnp.concatenate([every, extra])
        joined = jax.random.permutation(third, joined)
        return joined.reshape(NB_DEV, KR)
    return jax.vmap(one_partition)(keys).reshape(NB_DEV * NPART, KR).astype(jnp.int32)


def set_ends(drawn, rng, smallest, top_value):
    longest = drawn.shape.index(max(drawn.shape))
    spots = []
    for shift in (0, 1):
        where = [jax.random.randint(jax.random.fold_in(rng, axis), (), 0, length) for axis, length in enumerate(drawn.shape)]
        where[longest] = (where[longest] + shift) % drawn.shape[longest]
        spots.append(tuple(where))
    return drawn.at[spots[0]].set(smallest).at[spots[1]].set(top_value)


def shard_levels(own_key, extent, shards, smallest, largest):
    gain, own = 1.0, jax.random.fold_in(own_key, 6)
    for position, shards_of in shards:
        draws = jnp.exp(jax.random.uniform(jax.random.fold_in(own, position), (shards_of,), jnp.float32, smallest / len(shards), largest / len(shards)))
        gain = gain * jnp.repeat(draws, extent[position] // shards_of).reshape([-1 if axis == position else 1 for axis in range(len(extent))])
    return gain


def gaussian(key, extent, scale, bound, cuts=(), kind=jnp.bfloat16):
    array = scale * jax.random.normal(key, extent, jnp.float32)
    if cuts:
        array = array * shard_levels(key, extent, cuts, -0.22, 0.18)
    return jnp.clip(array, -bound, bound).astype(kind)


def setup_inputs(seed: int = 0, part: int = 0) -> dict:
    seeds = jax.random.split(jax.random.key(seed), 8)
    own_keys = jax.random.split(jax.random.fold_in(seeds[7], part), 8)
    features = gaussian(own_keys[0], (NODES, F), 1.0, 6.0, ((0, 16),))
    block_tiles = gaussian(own_keys[1], (NBLOCKS, BS, KR, BS), (KR * BS) ** -0.5, 0.078125, ((0, 16),))
    block_cols = draw_block_cols(jax.random.fold_in(jax.random.fold_in(seeds[7], part), 71), part)
    halo_request = set_ends(jax.random.randint(own_keys[3], (NPART, NPART), 0, NB_DEV), jax.random.fold_in(own_keys[3], 1), 0, NB_DEV - 1).astype(jnp.int32)
    labels = set_ends(jax.random.randint(own_keys[4], (NODES,), 0, C), jax.random.fold_in(own_keys[4], 1), 0, C - 1).astype(jnp.int32)
    weight_one = gaussian(seeds[5], (F, H), F ** -0.5, 0.5)
    weight_two = gaussian(seeds[6], (H, C), H ** -0.5, 0.375)
    return {"features": features, "block_tiles": block_tiles, "block_cols": block_cols, "halo_request": halo_request, "labels": labels, "weight_one": weight_one, "weight_two": weight_two}


def split_parts(value):
    high = lax.optimization_barrier(value.astype(jnp.bfloat16))
    low = (value - high.astype(jnp.float32)).astype(jnp.bfloat16)
    return (high, low)

def dot_right(left, value):
    high, low = split_parts(value)
    return jnp.dot(left, high, preferred_element_type=jnp.float32) + jnp.dot(left, low, preferred_element_type=jnp.float32)

def dot_left(value, right):
    high, low = split_parts(value)
    return jnp.dot(high, right, preferred_element_type=jnp.float32) + jnp.dot(low, right, preferred_element_type=jnp.float32)

def global_cols(block_cols, halo_request):
    rows = jnp.arange(NBLOCKS, dtype=jnp.int32)
    owner = rows // NB_DEV
    local_index = owner[:, None] * NB_DEV + block_cols
    peer = jnp.clip(block_cols - NB_DEV, 0, NPART - 1).astype(jnp.int32)
    remote = peer * NB_DEV + halo_request[owner[:, None], peer]
    return jnp.where(block_cols < NB_DEV, local_index, remote).astype(jnp.int32)

def aggregate(block_tiles, columns, values, exact):
    width = values.shape[1]
    blocks = values.reshape(NBLOCKS, BS, width)

    def one_row(index):
        taken = blocks[columns[index]].reshape(KR * BS, width)
        tile = block_tiles[index].reshape(BS, KR * BS)
        if exact:
            return dot_right(tile, taken)
        return jnp.dot(tile, taken, preferred_element_type=jnp.float32)
    return lax.map(one_row, jnp.arange(NBLOCKS, dtype=jnp.int32)).reshape(NODES, width)

def reference(features, block_tiles, block_cols, halo_request, labels, weight_one, weight_two):
    columns = global_cols(block_cols, halo_request)
    aggregated = aggregate(block_tiles, columns, features, False).astype(jnp.bfloat16)
    pre_one = jnp.dot(aggregated, weight_one, preferred_element_type=jnp.float32)
    hidden = jnp.maximum(pre_one, 0.0).astype(jnp.bfloat16)
    product = jnp.dot(hidden, weight_two, preferred_element_type=jnp.float32)
    logits = aggregate(block_tiles, columns, product, True)
    top = lax.optimization_barrier(jnp.max(logits, axis=1, keepdims=True))
    expo = jnp.exp(logits - top)
    probs = expo / lax.optimization_barrier(jnp.sum(expo, axis=1, keepdims=True))
    onehot = (labels[:, None] == jnp.arange(C, dtype=jnp.int32)[None, :]).astype(jnp.float32)
    grad_logits = (probs - onehot) / jnp.sqrt(jnp.float32(NODES))
    grad_blocks = grad_logits.reshape(NBLOCKS, BS, C)

    def back_row(carry, index):
        tile = block_tiles[index].reshape(BS, KR * BS)
        terms = dot_right(tile.T, grad_blocks[index]).reshape(KR, BS, C)
        return (carry.at[columns[index]].add(terms), None)
    start = jnp.zeros((NBLOCKS, BS, C), jnp.float32)
    grad_product, _ = lax.scan(back_row, start, jnp.arange(NBLOCKS, dtype=jnp.int32))
    grad_product = grad_product.reshape(NODES, C)
    grad_two = dot_right(hidden.T, grad_product)
    grad_hidden = dot_left(grad_product, weight_two.T)
    grad_pre = jnp.where(pre_one > 0.0, grad_hidden, 0.0)
    grad_one = dot_right(aggregated.T, grad_pre)
    return (logits, grad_one, grad_two)
```

```python
import functools
import math

import jax
import jax.numpy as jnp
from jax import lax
from jax.experimental import pallas as pl
from jax.experimental.pallas import tpu as pltpu
from jax.sharding import PartitionSpec as P

F32 = jnp.float32
BF16 = jnp.bfloat16
NT = (((1,), (1,)), ((), ()))


def dot(left, right):
    return jnp.dot(left, right, preferred_element_type=F32)


def dot_nt(left, right):
    return lax.dot_general(left, right, NT, preferred_element_type=F32)


def split_rows(value):
    high = value.astype(BF16)
    low = (value - high.astype(F32)).astype(BF16)
    return jnp.concatenate([high, low], axis=0)


def fold_rows(value, rows):
    return value[:rows] + value[rows:]


def merge_kernel(table, kr, cols_ref, tiles_ref, out_ref, acc):
    row = pl.program_id(0)
    bs = tiles_ref.shape[2]

    def clear(c, _):
        acc[c] = jnp.zeros((bs, bs), F32)
        return 0

    lax.fori_loop(0, table, clear, 0, unroll=2)

    def add(k, _):
        c = cols_ref[row, k]
        acc[c] += tiles_ref[0, k].astype(F32)
        return 0

    lax.fori_loop(0, kr, add, 0, unroll=4)

    def put(c, _):
        out_ref[:, pl.ds(pl.multiple_of(c * bs, bs), bs)] = acc[c].astype(BF16)
        return 0

    lax.fori_loop(0, table, put, 0, unroll=2)


def merge(tiles, cols, table):
    count, kr, bs, _ = tiles.shape
    return pl.pallas_call(
        functools.partial(merge_kernel, table, kr),
        out_shape=jax.ShapeDtypeStruct((count * bs, table * bs), BF16),
        grid_spec=pltpu.PrefetchScalarGridSpec(
            num_scalar_prefetch=1,
            grid=(count,),
            in_specs=[pl.BlockSpec((1, kr, bs, bs), lambda i, c: (i, 0, 0, 0))],
            out_specs=pl.BlockSpec((bs, table * bs), lambda i, c: (i, 0)),
            scratch_shapes=[pltpu.VMEM((table, bs, bs), F32)],
        ),
        compiler_params=pltpu.CompilerParams(vmem_limit_bytes=48 * 1024 * 1024),
        name="merge_tiles",
    )(cols, tiles)


def main_kernel(
    parts, count, bs, classes, cp, rp, nodes,
    req_ref, cols_ref, tiles_hbm, feat_ref, adj_ref, lab_ref, w1t_ref, w2t_ref, w2w_ref,
    logits_ref, one_ref, two_ref,
    idx_out, idx_in, stage, feat_in, prod_in, back_in, grads, grads_in, final,
    tiles, agg, hid, gate, prod, parts_hl, own_acc,
    tile_sem, send_sem, idx_sem, feat_sem, prod_sem, back_sem, rs_sem, ag_sem,
):
    grp = lax.axis_index("grp")
    me = lax.axis_index("dom")
    chips = parts // 2
    kr = tiles.shape[1]
    my_chip = me // 2
    own = count * bs

    def peer_at(s):
        return lax.rem(me + s, parts)

    def send(src, dst, sem, peer):
        return pltpu.make_async_remote_copy(
            src_ref=src, dst_ref=dst, send_sem=send_sem.at[peer], recv_sem=sem.at[me],
            device_id=(grp, peer), device_id_type=pl.DeviceIdType.MESH,
        )

    def arrival(buffer, sem, peer):
        return pltpu.make_async_remote_copy(
            src_ref=buffer, dst_ref=buffer, send_sem=send_sem.at[peer], recv_sem=sem.at[peer],
            device_id=(grp, peer), device_id_type=pl.DeviceIdType.MESH,
        )

    def each_peer(body):
        def step(s, _):
            body(peer_at(s))
            return 0

        lax.fori_loop(1, parts, step, 0)

    def each_chip(body):
        def step(s, _):
            body(lax.rem(my_chip + s, chips))
            return 0

        lax.fori_loop(0, chips, step, 0)

    def landed(buffer, sem, peer):
        @pl.when(peer != me)
        def _():
            arrival(buffer, sem, peer).wait_recv()

    def tile_copy(row):
        return pltpu.make_async_copy(tiles_hbm.at[row], tiles.at[row], tile_sem.at[row])

    for row in range(count):
        tile_copy(row).start()

    barrier = pltpu.get_barrier_semaphore()
    each_peer(lambda peer: pl.semaphore_signal(
        barrier, inc=1, device_id=(grp, peer), device_id_type=pl.DeviceIdType.MESH))
    pl.semaphore_wait(barrier, parts - 1)

    def ask(s, _):
        peer = peer_at(s)
        idx_out[peer] = jnp.full((8, 128), req_ref[0, peer], jnp.int32)
        send(idx_out.at[peer], idx_in.at[me], idx_sem, peer).start()
        return 0

    lax.fori_loop(1, parts, ask, 0)
    idx_in[me] = jnp.full((8, 128), req_ref[0, me], jnp.int32)

    def pick(peer, blocks):
        wanted = jnp.broadcast_to(idx_in[peer][:1], blocks[0].shape)
        out = blocks[0]
        for b in range(1, count):
            out = jnp.where(wanted == b, blocks[b], out)
        return out

    each_peer(lambda peer: send(idx_out.at[peer], idx_in.at[me], idx_sem, peer).wait_send())

    def send_features(peer):
        arrival(idx_in.at[peer], idx_sem, peer).wait_recv()
        blocks = [feat_ref[b * bs:(b + 1) * bs, :].astype(F32) for b in range(count)]
        stage[peer, 0:bs, :] = pick(peer, blocks).astype(BF16)
        send(stage.at[peer, 0:bs, :], feat_in.at[count + me], feat_sem, peer).start()

    each_peer(send_features)
    blocks = [feat_ref[b * bs:(b + 1) * bs, :].astype(F32) for b in range(count)]
    feat_in[count + me] = pick(me, blocks).astype(BF16)
    for b in range(count):
        feat_in[b] = feat_ref[b * bs:(b + 1) * bs, :]

    each_peer(lambda peer: arrival(feat_in.at[count + peer], feat_sem, peer).wait_recv())

    def aggregate_row(row, _):
        tile_copy(row).wait()
        total = jnp.zeros((bs, feat_ref.shape[1]), F32)
        for k in range(0, kr, 2):
            pair = jnp.concatenate(
                [feat_in[cols_ref[row, k]], feat_in[cols_ref[row, k + 1]]], axis=0)
            total += dot(jnp.concatenate([tiles[row, k], tiles[row, k + 1]], axis=1), pair)
        agg[pl.ds(pl.multiple_of(row * bs, bs), bs), :] = total.astype(BF16)
        return 0

    lax.fori_loop(0, count, aggregate_row, 0)
    each_peer(lambda peer: send(
        stage.at[peer, 0:bs, :], feat_in.at[count + me], feat_sem, peer).wait_send())

    pre = dot_nt(w1t_ref[...], agg[...])
    gate[...] = jnp.where(pre > 0.0, 1.0, 0.0).astype(F32)
    hid[...] = jnp.maximum(pre, 0.0).astype(BF16)
    prod[...] = dot(w2t_ref[...], hid[...])

    def product_block(peer):
        return pick(peer, [prod[:, b * bs:(b + 1) * bs] for b in range(count)]).astype(BF16)

    def send_product(peer):
        stage[peer] = product_block(peer)
        send(stage.at[peer], prod_in.at[me], prod_sem, peer).start()

    each_peer(send_product)
    prod_in[me] = product_block(me)

    parts_hl[...] = split_rows(prod[...])
    own_acc[...] = fold_rows(dot_nt(parts_hl[...], adj_ref[:, 0:own]), cp)

    def add_product(chip):
        landed(prod_in.at[2 * chip], prod_sem, 2 * chip)
        landed(prod_in.at[2 * chip + 1], prod_sem, 2 * chip + 1)
        pair = jnp.concatenate([prod_in[2 * chip], prod_in[2 * chip + 1]], axis=1)
        cols = adj_ref[:, pl.ds(pl.multiple_of(own + chip * 2 * bs, 128), 2 * bs)]
        own_acc[...] += dot_nt(pair, cols)

    each_chip(add_product)
    each_peer(lambda peer: send(stage.at[peer], prod_in.at[me], prod_sem, peer).wait_send())

    logits = own_acc[...]
    logits_ref[...] = logits[:classes]
    rows = lax.broadcasted_iota(jnp.int32, (cp, own), 0)
    real = rows < classes
    top = jnp.max(jnp.where(real, logits, -jnp.inf), axis=0, keepdims=True)
    expo = jnp.where(real, jnp.exp(logits - top), 0.0)
    probs = expo / jnp.sum(expo, axis=0, keepdims=True)
    onehot = jnp.where(rows == lab_ref[...], 1.0, 0.0)
    parts_hl[...] = split_rows((probs - onehot) / math.sqrt(nodes))

    def send_back(chip):
        cols = adj_ref[:, pl.ds(pl.multiple_of(own + chip * 2 * bs, 128), 2 * bs)]
        pair = fold_rows(dot(parts_hl[...], cols), cp).astype(BF16)
        for core in range(2):
            peer = 2 * chip + core
            block = pair[:, core * bs:(core + 1) * bs]

            @pl.when(peer != me)
            def _():
                stage[peer] = block
                send(stage.at[peer], back_in.at[me], back_sem, peer).start()

            @pl.when(peer == me)
            def _():
                back_in[peer] = block

    each_chip(send_back)
    own_acc[...] = fold_rows(dot(parts_hl[...], adj_ref[:, 0:own]), cp)

    def add_back(chip):
        for core in range(2):
            peer = 2 * chip + core
            landed(back_in.at[peer], back_sem, peer)
            block = back_in[peer].astype(F32)
            wanted = jnp.broadcast_to(idx_in[peer][:1], (cp, bs))
            for b in range(count):
                own_acc[:, b * bs:(b + 1) * bs] += jnp.where(wanted == b, block, 0.0)

    each_chip(add_back)
    each_peer(lambda peer: send(stage.at[peer], back_in.at[me], back_sem, peer).wait_send())

    split = split_rows(own_acc[...])
    parts_hl[...] = split
    two = fold_rows(dot_nt(split, hid[...]), cp)
    grad_pre = dot(w2w_ref[...], parts_hl[...]) * gate[...]
    one = fold_rows(dot(split_rows(grad_pre), agg[...]), hid.shape[0])
    hidden = hid.shape[0]
    halves = hidden // 128
    used = halves * cp + hidden
    for h in range(halves):
        grads[h * cp:(h + 1) * cp, :] = two[:, h * 128:(h + 1) * 128]
    grads[halves * cp:used, :] = one
    if used < parts * rp:
        grads[used:, :] = jnp.zeros((parts * rp - used, 128), F32)

    def share(peer):
        return pl.ds(pl.multiple_of(peer * rp, 8), rp)

    each_peer(lambda peer: send(
        grads.at[share(peer)], grads_in.at[me], rs_sem, peer).start())
    grads_in[me] = grads[share(me)]

    def take(peer):
        arrival(grads_in.at[peer], rs_sem, peer).wait_recv()

    each_peer(take)
    each_peer(lambda peer: send(
        grads.at[share(peer)], grads_in.at[me], rs_sem, peer).wait_send())
    total = lax.fori_loop(0, parts, lambda p, t: t + grads_in[p], jnp.zeros((rp, 128), F32))
    final[share(me)] = total
    each_peer(lambda peer: send(
        final.at[share(me)], final.at[share(me)], ag_sem, peer).start())

    def take_total(peer):
        arrival(final.at[share(peer)], ag_sem, peer).wait_recv()

    each_peer(take_total)
    each_peer(lambda peer: send(
        final.at[share(me)], final.at[share(me)], ag_sem, peer).wait_send())
    for h in range(halves):
        two_ref[:, h * 128:(h + 1) * 128] = final[h * cp:h * cp + classes, :]
    one_ref[...] = final[halves * cp:used, :].T


def local(features, block_tiles, block_cols, halo_request, labels, weight_one, weight_two):
    parts = lax.axis_size("dom")
    count, bs, kr, _ = block_tiles.shape
    width = features.shape[1]
    hidden, classes = weight_two.shape
    cp = -(-classes // 16) * 16
    own = count * bs
    table = count + parts
    used = (hidden // 128) * cp + hidden
    rp = -(-used // (8 * parts)) * 8
    tiles = block_tiles.transpose(0, 2, 1, 3)
    adj = merge(tiles, block_cols, table)
    w2t = jnp.pad(weight_two.T, ((0, cp - classes), (0, 0)))
    w2w = jnp.pad(weight_two, ((0, 0), (0, cp - classes)))
    w2w = jnp.concatenate([w2w, w2w], axis=1)
    vmem = pl.BlockSpec(memory_space=pltpu.VMEM)
    smem = pl.BlockSpec(memory_space=pltpu.SMEM)
    dma = pltpu.SemaphoreType.DMA((parts,))
    logits, one, two = pl.pallas_call(
        functools.partial(main_kernel, parts, count, bs, classes, cp, rp, parts * own),
        out_shape=(
            jax.ShapeDtypeStruct((classes, own), F32),
            jax.ShapeDtypeStruct((width, hidden), F32),
            jax.ShapeDtypeStruct((classes, hidden), F32),
        ),
        in_specs=[smem, smem, pl.BlockSpec(memory_space=pl.ANY)] + [vmem] * 6,
        out_specs=(vmem, vmem, vmem),
        scratch_shapes=[
            pltpu.VMEM((parts, 8, 128), jnp.int32),
            pltpu.VMEM((parts, 8, 128), jnp.int32),
            pltpu.VMEM((parts, cp, bs), BF16),
            pltpu.VMEM((table, bs, width), BF16),
            pltpu.VMEM((parts, cp, bs), BF16),
            pltpu.VMEM((parts, cp, bs), BF16),
            pltpu.VMEM((parts * rp, 128), F32),
            pltpu.VMEM((parts, rp, 128), F32),
            pltpu.VMEM((parts * rp, 128), F32),
            pltpu.VMEM((count, kr, bs, bs), BF16),
            pltpu.VMEM((own, width), BF16),
            pltpu.VMEM((hidden, own), BF16),
            pltpu.VMEM((hidden, own), F32),
            pltpu.VMEM((cp, own), F32),
            pltpu.VMEM((2 * cp, own), BF16),
            pltpu.VMEM((cp, own), F32),
            pltpu.SemaphoreType.DMA((count,)),
            dma, dma, dma, dma, dma, dma, dma,
        ],
        compiler_params=pltpu.CompilerParams(
            collective_id=0, has_side_effects=True, vmem_limit_bytes=63 * 1024 * 1024),
        name="graph_layers",
    )(halo_request, block_cols, tiles, features, adj, labels.reshape(1, own), weight_one.T, w2t, w2w)
    return (logits.T, one, two.T)


def solution(mesh):
    placed = (
        P(("grp", "dom"), None),
        P(("grp", "dom"), None, None, None),
        P(("grp", "dom"), None),
        P(("grp", "dom"), None),
        P(("grp", "dom")),
        P(),
        P(),
    )
    return jax.shard_map(
        local,
        mesh=mesh,
        in_specs=placed,
        out_specs=(P(("grp", "dom"), None), P("grp", None), P("grp", None)),
        check_vma=False,
    )
```

```python
import functools
import math

import jax
import jax.numpy as jnp
from jax import lax
from jax.experimental import pallas as pl
from jax.experimental.pallas import tpu as pltpu
from jax.sharding import PartitionSpec as P

F32 = jnp.float32
BF16 = jnp.bfloat16
NT = (((1,), (1,)), ((), ()))


def dot(left, right):
    return jnp.dot(left, right, preferred_element_type=F32)


def dot_nt(left, right):
    return lax.dot_general(left, right, NT, preferred_element_type=F32)


def split_rows(value):
    high = value.astype(BF16)
    low = (value - high.astype(F32)).astype(BF16)
    return jnp.concatenate([high, low], axis=0)


def fold_rows(value, rows):
    return value[:rows] + value[rows:]


def main_kernel(
    parts, count, kr, bs, classes, cp, rp, nodes,
    req_ref, cols_ref, prev_ref, last_ref, tiles_hbm, feat_ref, lab_ref, w1_ref, w2t_ref,
    logits_ref, sums_ref,
    idx_out, idx_in, stage, feat_tab, agg_tab, tiles, chain, adj,
    grads, grads_in, final, w1t, w2pad, w2t, w2, acc, g_hl, two_acc, one_acc,
    tile_sem, send_sem, idx_sem, feat_sem, agg_sem, rs_sem, ag_sem,
):
    grp = lax.axis_index("grp")
    me = lax.axis_index("dom")
    chips = parts // 2
    my_chip = me // 2
    own_pairs = count // 2
    table = count + parts
    own = count * bs
    hidden = w1_ref.shape[1]
    halves = hidden // 128
    used = halves * cp + hidden

    def peer_at(s):
        return lax.rem(me + s, parts)

    def send(src, dst, sem, peer):
        return pltpu.make_async_remote_copy(
            src_ref=src, dst_ref=dst, send_sem=send_sem.at[peer], recv_sem=sem.at[me],
            device_id=(grp, peer), device_id_type=pl.DeviceIdType.MESH,
        )

    def arrival(buffer, sem, peer):
        return pltpu.make_async_remote_copy(
            src_ref=buffer, dst_ref=buffer, send_sem=send_sem.at[peer], recv_sem=sem.at[peer],
            device_id=(grp, peer), device_id_type=pl.DeviceIdType.MESH,
        )

    def each_peer(body):
        def step(s, _):
            body(peer_at(s))
            return 0

        lax.fori_loop(1, parts, step, 0)

    def tile_copy(row):
        return pltpu.make_async_copy(tiles_hbm.at[row], tiles.at[row], tile_sem.at[row])

    for row in range(count):
        tile_copy(row).start()

    barrier = pltpu.get_barrier_semaphore()
    each_peer(lambda peer: pl.semaphore_signal(
        barrier, inc=1, device_id=(grp, peer), device_id_type=pl.DeviceIdType.MESH))
    pl.semaphore_wait(barrier, parts - 1)

    def ask(s, _):
        peer = peer_at(s)
        idx_out[peer] = jnp.full((8, 128), req_ref[0, peer], jnp.int32)
        send(idx_out.at[peer], idx_in.at[me], idx_sem, peer).start()
        return 0

    lax.fori_loop(1, parts, ask, 0)
    idx_in[me] = jnp.full((8, 128), req_ref[0, me], jnp.int32)
    w1t[...] = w1_ref[...].astype(F32).T.astype(BF16)
    w2pad[...] = jnp.zeros(w2pad.shape, F32)
    w2pad[0:classes, :] = w2t_ref[...].astype(F32)
    w2t[...] = w2pad[0:cp, :].astype(BF16)
    w2[...] = w2pad[...].T[:, 0:cp].astype(BF16)
    for b in range(count):
        feat_tab[b] = feat_ref[b * bs:(b + 1) * bs, :]
    each_peer(lambda peer: send(idx_out.at[peer], idx_in.at[me], idx_sem, peer).wait_send())

    def pick(peer, tab):
        wanted = jnp.broadcast_to(idx_in[peer][:1], tab.shape[1:])
        out = tab[0].astype(F32)
        for b in range(1, count):
            out = jnp.where(wanted == b, tab[b].astype(F32), out)
        return out.astype(BF16)

    def exchange(tab, sem, first):
        def go(peer):
            if first:
                arrival(idx_in.at[peer], idx_sem, peer).wait_recv()
            stage[peer] = pick(peer, tab)
            send(stage.at[peer], tab.at[count + me], sem, peer).start()

        each_peer(go)
        tab[count + me] = pick(me, tab)

    def sent(tab, sem):
        each_peer(lambda peer: send(stage.at[peer], tab.at[count + me], sem, peer).wait_send())

    exchange(feat_tab, feat_sem, True)

    chain[0] = jnp.zeros((bs, bs), F32)

    def merge_row(row, _):
        tile_copy(row).wait()

        def add(k, _):
            chain[k + 1] = tiles[row, k].astype(F32) + chain[prev_ref[row, k]]
            return 0

        lax.fori_loop(0, kr, add, 0, unroll=4)
        rows = pl.ds(pl.multiple_of(row * bs, bs), bs)

        def put(c, _):
            adj[rows, pl.ds(pl.multiple_of(c * bs, bs), bs)] = chain[last_ref[row, c]].astype(BF16)
            return 0

        lax.fori_loop(0, table, put, 0, unroll=2)
        return 0

    lax.fori_loop(0, count, merge_row, 0)

    each_peer(lambda peer: arrival(feat_tab.at[count + peer], feat_sem, peer).wait_recv())

    def aggregate_row(row, _):
        total = jnp.zeros((bs, feat_ref.shape[1]), F32)
        for k in range(0, kr, 2):
            pair = jnp.concatenate(
                [feat_tab[cols_ref[row, k]], feat_tab[cols_ref[row, k + 1]]], axis=0)
            total += dot(jnp.concatenate([tiles[row, k], tiles[row, k + 1]], axis=1), pair)
        agg_tab[row] = total.astype(BF16)
        return 0

    lax.fori_loop(0, count, aggregate_row, 0)
    sent(feat_tab, feat_sem)

    exchange(agg_tab, agg_sem, False)

    def pair_cols(j):
        return adj[:, pl.ds(pl.multiple_of(j * 2 * bs, 2 * bs), 2 * bs)]

    def pair_agg(j):
        return agg_tab[pl.ds(2 * j, 2)].reshape(2 * bs, w1_ref.shape[0])

    def forward(j):
        pre = dot_nt(w1t[...], pair_agg(j))
        prod = dot(w2t[...], jnp.maximum(pre, 0.0).astype(BF16))
        return fold_rows(dot_nt(split_rows(prod), pair_cols(j)), cp)

    acc[...] = forward(0)
    for j in range(1, own_pairs):
        acc[...] += forward(j)

    def halo(s, _):
        chip = lax.rem(my_chip + s, chips)
        for core in range(2):
            peer = 2 * chip + core

            @pl.when(peer != me)
            def _():
                arrival(agg_tab.at[count + peer], agg_sem, peer).wait_recv()

        acc[...] += forward(own_pairs + chip)
        return 0

    lax.fori_loop(0, chips, halo, 0)
    sent(agg_tab, agg_sem)

    logits = acc[...]
    logits_ref[...] = logits
    rows = lax.broadcasted_iota(jnp.int32, (cp, own), 0)
    real = rows < classes
    top = jnp.max(jnp.where(real, logits, -jnp.inf), axis=0, keepdims=True)
    expo = jnp.where(real, jnp.exp(logits - top), 0.0)
    probs = expo / jnp.sum(expo, axis=0, keepdims=True)
    labels = jnp.concatenate([lab_ref[b:b + 1, :] for b in range(count)], axis=1)
    onehot = jnp.where(rows == labels, 1.0, 0.0)
    g_hl[...] = split_rows((probs - onehot) / math.sqrt(nodes))

    two_acc[...] = jnp.zeros(two_acc.shape, F32)
    one_acc[...] = jnp.zeros(one_acc.shape, F32)

    def backward(j, _):
        agg = pair_agg(j)
        pre = dot_nt(w1t[...], agg)
        term = split_rows(fold_rows(dot(g_hl[...], pair_cols(j)), cp))
        two_acc[...] += fold_rows(dot_nt(term, jnp.maximum(pre, 0.0).astype(BF16)), cp)
        grad_hidden = dot(w2[...], term[:cp]) + dot(w2[...], term[cp:])
        grad_pre = jnp.where(pre > 0.0, grad_hidden, 0.0)
        one_acc[...] += fold_rows(dot(split_rows(grad_pre), agg), hidden)
        return 0

    lax.fori_loop(0, table // 2, backward, 0, unroll=table <= 32)

    for h in range(halves):
        grads[h * cp:(h + 1) * cp, :] = two_acc[:, h * 128:(h + 1) * 128]
    grads[halves * cp:used, :] = one_acc[...]
    if used < parts * rp:
        grads[used:, :] = jnp.zeros((parts * rp - used, 128), F32)

    def share(peer):
        return pl.ds(pl.multiple_of(peer * rp, 8), rp)

    each_peer(lambda peer: send(
        grads.at[share(peer)], grads_in.at[me], rs_sem, peer).start())
    grads_in[me] = grads[share(me)]

    def take(peer):
        arrival(grads_in.at[peer], rs_sem, peer).wait_recv()

    each_peer(take)
    each_peer(lambda peer: send(
        grads.at[share(peer)], grads_in.at[me], rs_sem, peer).wait_send())
    total = lax.fori_loop(0, parts, lambda p, t: t + grads_in[p], jnp.zeros((rp, 128), F32))
    final[share(me)] = total
    each_peer(lambda peer: send(
        final.at[share(me)], final.at[share(me)], ag_sem, peer).start())

    def take_total(peer):
        arrival(final.at[share(peer)], ag_sem, peer).wait_recv()

    each_peer(take_total)
    each_peer(lambda peer: send(
        final.at[share(me)], final.at[share(me)], ag_sem, peer).wait_send())
    sums_ref[...] = final[0:used, :]


def place_kernel(classes, cp, hidden, logits_ref, sums_ref, out_ref, one_ref, two_ref):
    halves = hidden // 128
    out_ref[...] = logits_ref[0:classes, :]
    for h in range(halves):
        two_ref[:, h * 128:(h + 1) * 128] = sums_ref[h * cp:h * cp + classes, :]
    one_ref[...] = sums_ref[halves * cp:, :].T


def local(features, block_tiles, block_cols, halo_request, labels, weight_one, weight_two):
    parts = lax.axis_size("dom")
    count, bs, kr, _ = block_tiles.shape
    width = features.shape[1]
    hidden, classes = weight_two.shape
    cp = -(-classes // 16) * 16
    cw = -(-classes // 128) * 128
    own = count * bs
    table = count + parts
    used = (hidden // 128) * cp + hidden
    rp = -(-used // (8 * parts)) * 8
    tiles = block_tiles.transpose(0, 2, 1, 3)
    slot = jnp.arange(kr, dtype=jnp.int32)
    same = block_cols[:, :, None] == block_cols[:, None, :]
    before = slot[None, None, :] < slot[None, :, None]
    prev = jnp.max(jnp.where(same & before, slot[None, None, :] + 1, 0), axis=2)
    here = block_cols[:, None, :] == jnp.arange(table, dtype=jnp.int32)[None, :, None]
    last = jnp.max(jnp.where(here, slot[None, None, :] + 1, 0), axis=2)
    vmem = pl.BlockSpec(memory_space=pltpu.VMEM)
    smem = pl.BlockSpec(memory_space=pltpu.SMEM)
    dma = pltpu.SemaphoreType.DMA((parts,))
    logits, sums = pl.pallas_call(
        functools.partial(main_kernel, parts, count, kr, bs, classes, cp, rp, parts * own),
        out_shape=(
            jax.ShapeDtypeStruct((cp, own), F32),
            jax.ShapeDtypeStruct((used, 128), F32),
        ),
        in_specs=[smem] * 4 + [pl.BlockSpec(memory_space=pl.ANY)] + [vmem] * 4,
        out_specs=(vmem, vmem),
        scratch_shapes=[
            pltpu.VMEM((parts, 8, 128), jnp.int32),
            pltpu.VMEM((parts, 8, 128), jnp.int32),
            pltpu.VMEM((parts, bs, width), BF16),
            pltpu.VMEM((table, bs, width), BF16),
            pltpu.VMEM((table, bs, width), BF16),
            pltpu.VMEM((count, kr, bs, bs), BF16),
            pltpu.VMEM((kr + 1, bs, bs), F32),
            pltpu.VMEM((own, table * bs), BF16),
            pltpu.VMEM((parts * rp, 128), F32),
            pltpu.VMEM((parts, rp, 128), F32),
            pltpu.VMEM((parts * rp, 128), F32),
            pltpu.VMEM((hidden, width), BF16),
            pltpu.VMEM((cw, hidden), F32),
            pltpu.VMEM((cp, hidden), BF16),
            pltpu.VMEM((hidden, cp), BF16),
            pltpu.VMEM((cp, own), F32),
            pltpu.VMEM((2 * cp, own), BF16),
            pltpu.VMEM((cp, hidden), F32),
            pltpu.VMEM((hidden, width), F32),
            pltpu.SemaphoreType.DMA((count,)),
            dma, dma, dma, dma, dma, dma,
        ],
        compiler_params=pltpu.CompilerParams(
            collective_id=0, has_side_effects=True, vmem_limit_bytes=62 * 1024 * 1024),
        name="graph_layers",
    )(halo_request, block_cols, prev, last, tiles, features, labels.reshape(count, bs),
      weight_one, weight_two.T)
    logits, one, two = pl.pallas_call(
        functools.partial(place_kernel, classes, cp, hidden),
        out_shape=(
            jax.ShapeDtypeStruct((classes, own), F32),
            jax.ShapeDtypeStruct((width, hidden), F32),
            jax.ShapeDtypeStruct((classes, hidden), F32),
        ),
        in_specs=[vmem, vmem],
        out_specs=(vmem, vmem, vmem),
        name="place_results",
    )(logits, sums)
    return (logits.T, one, two.T)


def solution(mesh):
    placed = (
        P(("grp", "dom"), None),
        P(("grp", "dom"), None, None, None),
        P(("grp", "dom"), None),
        P(("grp", "dom"), None),
        P(("grp", "dom")),
        P(),
        P(),
    )
    return jax.shard_map(
        local,
        mesh=mesh,
        in_specs=placed,
        out_specs=(P(("grp", "dom"), None), P("grp", None), P("grp", None)),
        check_vma=False,
    )
```

```python
import functools
import math

import jax
import jax.numpy as jnp
from jax import lax
from jax.experimental import pallas as pl
from jax.experimental.pallas import tpu as pltpu
from jax.sharding import PartitionSpec as P

F32 = jnp.float32
BF16 = jnp.bfloat16
NT = (((1,), (1,)), ((), ()))


def dot(left, right):
    return jnp.dot(left, right, preferred_element_type=F32)


def dot_nt(left, right):
    return lax.dot_general(left, right, NT, preferred_element_type=F32)


def split_rows(value):
    high = value.astype(BF16)
    low = (value - high.astype(F32)).astype(BF16)
    return jnp.concatenate([high, low], axis=0)


def fold_rows(value, rows):
    return value[:rows] + value[rows:]


def main_kernel(
    parts, count, kr, bs, classes, cp, rp, nodes,
    req_ref, cols_ref, colv_ref, tiles_hbm, feat_ref, lab_ref, w1_ref, w2t_ref,
    logits_ref, sums_ref,
    idx_out, idx_in, stage, feat_tab, agg_tab, tiles, chain, adj,
    grads, grads_in, final, w1t, w2pad, w2t, w2, acc, g_hl, two_acc, one_acc,
    plan_v, plan_s, plan_sem, tile_sem, send_sem, idx_sem, feat_sem, agg_sem, rs_sem, ag_sem,
):
    grp = lax.axis_index("grp")
    me = lax.axis_index("dom")
    chips = parts // 2
    my_chip = me // 2
    own_pairs = count // 2
    wide = -(-(count + parts) // 128)
    table = count + parts
    own = count * bs
    hidden = w1_ref.shape[1]
    halves = hidden // 128
    used = halves * cp + hidden

    def partner(place, t, n):
        if n & (n - 1):
            return lax.rem(place + t, n)
        out, bit = place, 1
        while bit < n:
            out += bit * lax.rem(lax.div(t, bit), 2) * (1 - 2 * lax.rem(lax.div(place, bit), 2))
            bit *= 2
        return out

    def send(src, dst, sem, peer):
        return pltpu.make_async_remote_copy(
            src_ref=src, dst_ref=dst, send_sem=send_sem.at[peer], recv_sem=sem.at[me],
            device_id=(grp, peer), device_id_type=pl.DeviceIdType.MESH,
        )

    def arrival(buffer, sem, peer):
        return pltpu.make_async_remote_copy(
            src_ref=buffer, dst_ref=buffer, send_sem=send_sem.at[peer], recv_sem=sem.at[peer],
            device_id=(grp, peer), device_id_type=pl.DeviceIdType.MESH,
        )

    def each_peer(body):
        def step(s, _):
            body(partner(me, parts - s, parts))
            return 0

        lax.fori_loop(1, parts, step, 0)

    def tile_copy(row):
        return pltpu.make_async_copy(tiles_hbm.at[row], tiles.at[row], tile_sem.at[row])

    for row in range(count):
        tile_copy(row).start()

    barrier = pltpu.get_barrier_semaphore()
    each_peer(lambda peer: pl.semaphore_signal(
        barrier, inc=1, device_id=(grp, peer), device_id_type=pl.DeviceIdType.MESH))
    w1t[...] = w1_ref[...].astype(F32).T.astype(BF16)
    w2pad[...] = jnp.zeros(w2pad.shape, F32)
    w2pad[0:classes, :] = w2t_ref[...].astype(F32)
    w2t[...] = w2pad[0:cp, :].astype(BF16)
    w2[...] = w2pad[...].T[:, 0:cp].astype(BF16)
    for b in range(count):
        feat_tab[b] = feat_ref[b * bs:(b + 1) * bs, :]
    slot = lax.broadcasted_iota(jnp.int32, (1, kr), 1)
    lane = lax.broadcasted_iota(jnp.int32, (1, 128), 1)
    plan_v[...] = jnp.zeros(plan_v.shape, jnp.int32)

    def plan_tile(k, held):
        out = []
        for row in range(count):
            col = cols_ref[row, k]
            prev, lasts = held[row][0], held[row][1:]
            same = jnp.logical_and(colv_ref[row:row + 1, :] == col, slot > k)
            new = [jnp.where(same, k + 1, prev)]
            for w in range(wide):
                new.append(jnp.where(lane + 128 * w == col, k + 1, lasts[w]))
            out.append(tuple(new))
        return tuple(out)

    none = (jnp.zeros((1, kr), jnp.int32),) + (jnp.zeros((1, 128), jnp.int32),) * wide
    plans = lax.fori_loop(0, kr, plan_tile, (none,) * count, unroll=4)
    for row in range(count):
        plan_v[row:row + 1, 0:kr] = plans[row][0]
        for w in range(wide):
            at = 8 * (1 + w) + row
            plan_v[at:at + 1, :] = plans[row][1 + w]
    plan_copy = pltpu.make_async_copy(plan_v, plan_s, plan_sem)
    plan_copy.start()
    plan_copy.wait()
    pl.semaphore_wait(barrier, parts - 1)

    def ask(peer):
        idx_out[peer] = jnp.full((8, 128), req_ref[0, peer], jnp.int32)
        send(idx_out.at[peer], idx_in.at[me], idx_sem, peer).start()

    each_peer(ask)
    idx_in[me] = jnp.full((8, 128), req_ref[0, me], jnp.int32)
    each_peer(lambda peer: send(idx_out.at[peer], idx_in.at[me], idx_sem, peer).wait_send())

    def pick(peer, tab):
        wanted = jnp.broadcast_to(idx_in[peer][:1], tab.shape[1:])
        out = tab[0].astype(F32)
        for b in range(1, count):
            out = jnp.where(wanted == b, tab[b].astype(F32), out)
        return out.astype(BF16)

    def exchange(tab, sem, first):
        def go(peer):
            if first:
                arrival(idx_in.at[peer], idx_sem, peer).wait_recv()
            stage[peer] = pick(peer, tab)
            send(stage.at[peer], tab.at[count + me], sem, peer).start()

        each_peer(go)
        tab[count + me] = pick(me, tab)

    def sent(tab, sem):
        each_peer(lambda peer: send(stage.at[peer], tab.at[count + me], sem, peer).wait_send())

    exchange(feat_tab, feat_sem, True)

    chain[0] = jnp.zeros((bs, bs), F32)

    def merge_row(row, _):
        tile_copy(row).wait()

        def add(k, _):
            chain[k + 1] = tiles[row, k].astype(F32) + chain[plan_s[row, k]]
            return 0

        lax.fori_loop(0, kr, add, 0, unroll=4)
        rows = pl.ds(pl.multiple_of(row * bs, bs), bs)

        def put(c, _):
            last = plan_s[8 * (1 + lax.div(c, 128)) + row, lax.rem(c, 128)]
            adj[rows, pl.ds(pl.multiple_of(c * bs, bs), bs)] = chain[last].astype(BF16)
            return 0

        lax.fori_loop(0, table, put, 0, unroll=2)
        return 0

    lax.fori_loop(0, count, merge_row, 0)

    each_peer(lambda peer: arrival(feat_tab.at[count + peer], feat_sem, peer).wait_recv())

    def aggregate_row(row, _):
        total = jnp.zeros((bs, feat_ref.shape[1]), F32)
        for k in range(0, kr, 2):
            pair = jnp.concatenate(
                [feat_tab[cols_ref[row, k]], feat_tab[cols_ref[row, k + 1]]], axis=0)
            total += dot(jnp.concatenate([tiles[row, k], tiles[row, k + 1]], axis=1), pair)
        agg_tab[row] = total.astype(BF16)
        return 0

    lax.fori_loop(0, count, aggregate_row, 0)
    sent(feat_tab, feat_sem)

    exchange(agg_tab, agg_sem, False)

    def pair_cols(j):
        return adj[:, pl.ds(pl.multiple_of(j * 2 * bs, 2 * bs), 2 * bs)]

    def pair_agg(j):
        return agg_tab[pl.ds(2 * j, 2)].reshape(2 * bs, w1_ref.shape[0])

    def forward(j):
        pre = dot_nt(w1t[...], pair_agg(j))
        prod = dot(w2t[...], jnp.maximum(pre, 0.0).astype(BF16))
        return fold_rows(dot_nt(split_rows(prod), pair_cols(j)), cp)

    acc[...] = forward(0)
    for j in range(1, own_pairs):
        acc[...] += forward(j)

    def halo(s, _):
        chip = partner(my_chip, s, chips)
        for core in range(2):
            peer = 2 * chip + core

            @pl.when(peer != me)
            def _():
                arrival(agg_tab.at[count + peer], agg_sem, peer).wait_recv()

        acc[...] += forward(own_pairs + chip)
        return 0

    lax.fori_loop(0, chips, halo, 0)
    sent(agg_tab, agg_sem)

    logits = acc[...]
    logits_ref[...] = logits
    rows = lax.broadcasted_iota(jnp.int32, (cp, own), 0)
    real = rows < classes
    top = jnp.max(jnp.where(real, logits, -jnp.inf), axis=0, keepdims=True)
    expo = jnp.where(real, jnp.exp(logits - top), 0.0)
    probs = expo / jnp.sum(expo, axis=0, keepdims=True)
    labels = jnp.concatenate([lab_ref[b:b + 1, :] for b in range(count)], axis=1)
    onehot = jnp.where(rows == labels, 1.0, 0.0)
    g_hl[...] = split_rows((probs - onehot) / math.sqrt(nodes))

    two_acc[...] = jnp.zeros(two_acc.shape, F32)
    one_acc[...] = jnp.zeros(one_acc.shape, F32)

    def backward(j, _):
        agg = pair_agg(j)
        pre = dot_nt(w1t[...], agg)
        term = split_rows(fold_rows(dot(g_hl[...], pair_cols(j)), cp))
        two_acc[...] += fold_rows(dot_nt(term, jnp.maximum(pre, 0.0).astype(BF16)), cp)
        grad_hidden = dot(w2[...], term[:cp]) + dot(w2[...], term[cp:])
        grad_pre = jnp.where(pre > 0.0, grad_hidden, 0.0)
        one_acc[...] += fold_rows(dot(split_rows(grad_pre), agg), hidden)
        return 0

    lax.fori_loop(0, table // 2, backward, 0, unroll=table <= 32)

    for h in range(halves):
        grads[h * cp:(h + 1) * cp, :] = two_acc[:, h * 128:(h + 1) * 128].astype(BF16)
    grads[halves * cp:used, :] = one_acc[...].astype(BF16)
    if used < parts * rp:
        grads[used:, :] = jnp.zeros((parts * rp - used, 128), BF16)

    def share(peer):
        return pl.ds(pl.multiple_of(peer * rp, 16), rp)

    each_peer(lambda peer: send(
        grads.at[share(peer)], grads_in.at[me], rs_sem, peer).start())
    grads_in[me] = grads[share(me)]

    def take(peer):
        arrival(grads_in.at[peer], rs_sem, peer).wait_recv()

    each_peer(take)
    each_peer(lambda peer: send(
        grads.at[share(peer)], grads_in.at[me], rs_sem, peer).wait_send())
    total = lax.fori_loop(0, parts, lambda p, t: t + grads_in[p].astype(F32), jnp.zeros((rp, 128), F32))
    final[share(me)] = total.astype(BF16)
    each_peer(lambda peer: send(
        final.at[share(me)], final.at[share(me)], ag_sem, peer).start())

    def take_total(peer):
        arrival(final.at[share(peer)], ag_sem, peer).wait_recv()

    each_peer(take_total)
    each_peer(lambda peer: send(
        final.at[share(me)], final.at[share(me)], ag_sem, peer).wait_send())
    sums_ref[...] = final[0:used, :].astype(F32)


def place_kernel(classes, cp, hidden, logits_ref, sums_ref, out_ref, one_ref, two_ref):
    halves = hidden // 128
    out_ref[...] = logits_ref[0:classes, :]
    for h in range(halves):
        two_ref[:, h * 128:(h + 1) * 128] = sums_ref[h * cp:h * cp + classes, :]
    one_ref[...] = sums_ref[halves * cp:, :].T


def local(features, block_tiles, block_cols, halo_request, labels, weight_one, weight_two):
    parts = lax.axis_size("dom")
    count, bs, kr, _ = block_tiles.shape
    width = features.shape[1]
    hidden, classes = weight_two.shape
    cp = -(-classes // 16) * 16
    cw = -(-classes // 128) * 128
    own = count * bs
    table = count + parts
    used = (hidden // 128) * cp + hidden
    rp = -(-used // (16 * parts)) * 16
    tiles = block_tiles.transpose(0, 2, 1, 3)
    plan = (8 * (1 + -(-table // 128)), 128)
    vmem = pl.BlockSpec(memory_space=pltpu.VMEM)
    smem = pl.BlockSpec(memory_space=pltpu.SMEM)
    dma = pltpu.SemaphoreType.DMA((parts,))
    logits, sums = pl.pallas_call(
        functools.partial(main_kernel, parts, count, kr, bs, classes, cp, rp, parts * own),
        out_shape=(
            jax.ShapeDtypeStruct((cp, own), F32),
            jax.ShapeDtypeStruct((used, 128), F32),
        ),
        in_specs=[smem, smem, vmem, pl.BlockSpec(memory_space=pl.ANY)] + [vmem] * 4,
        out_specs=(vmem, vmem),
        scratch_shapes=[
            pltpu.VMEM((parts, 8, 128), jnp.int32),
            pltpu.VMEM((parts, 8, 128), jnp.int32),
            pltpu.VMEM((parts, bs, width), BF16),
            pltpu.VMEM((table, bs, width), BF16),
            pltpu.VMEM((table, bs, width), BF16),
            pltpu.VMEM((count, kr, bs, bs), BF16),
            pltpu.VMEM((kr + 1, bs, bs), F32),
            pltpu.VMEM((own, table * bs), BF16),
            pltpu.VMEM((parts * rp, 128), BF16),
            pltpu.VMEM((parts, rp, 128), BF16),
            pltpu.VMEM((parts * rp, 128), BF16),
            pltpu.VMEM((hidden, width), BF16),
            pltpu.VMEM((cw, hidden), F32),
            pltpu.VMEM((cp, hidden), BF16),
            pltpu.VMEM((hidden, cp), BF16),
            pltpu.VMEM((cp, own), F32),
            pltpu.VMEM((2 * cp, own), BF16),
            pltpu.VMEM((cp, hidden), F32),
            pltpu.VMEM((hidden, width), F32),
            pltpu.VMEM(plan, jnp.int32),
            pltpu.SMEM(plan, jnp.int32),
            pltpu.SemaphoreType.DMA,
            pltpu.SemaphoreType.DMA((count,)),
            dma, dma, dma, dma, dma, dma,
        ],
        compiler_params=pltpu.CompilerParams(
            collective_id=0, has_side_effects=True, vmem_limit_bytes=62 * 1024 * 1024),
        name="graph_layers",
    )(halo_request, block_cols, block_cols, tiles, features, labels.reshape(count, bs),
      weight_one, weight_two.T)
    logits, one, two = pl.pallas_call(
        functools.partial(place_kernel, classes, cp, hidden),
        out_shape=(
            jax.ShapeDtypeStruct((classes, own), F32),
            jax.ShapeDtypeStruct((width, hidden), F32),
            jax.ShapeDtypeStruct((classes, hidden), F32),
        ),
        in_specs=[vmem, vmem],
        out_specs=(vmem, vmem, vmem),
        name="place_results",
    )(logits, sums)
    return (logits.T, one, two.T)


def solution(mesh):
    placed = (
        P(("grp", "dom"), None),
        P(("grp", "dom"), None, None, None),
        P(("grp", "dom"), None),
        P(("grp", "dom"), None),
        P(("grp", "dom")),
        P(),
        P(),
    )
    return jax.shard_map(
        local,
        mesh=mesh,
        in_specs=placed,
        out_specs=(P(("grp", "dom"), None), P("grp", None), P("grp", None)),
        check_vma=False,
    )
```

```python
import functools
import math

import jax
import jax.numpy as jnp
from jax import lax
from jax.experimental import pallas as pl
from jax.experimental.pallas import tpu as pltpu
from jax.sharding import PartitionSpec as P

F32 = jnp.float32
BF16 = jnp.bfloat16
NT = (((1,), (1,)), ((), ()))


def dot(left, right):
    return jnp.dot(left, right, preferred_element_type=F32)


def dot_nt(left, right):
    return lax.dot_general(left, right, NT, preferred_element_type=F32)


def split_rows(value):
    high = value.astype(BF16)
    low = (value - high.astype(F32)).astype(BF16)
    return jnp.concatenate([high, low], axis=0)


def fold_rows(value, rows):
    return value[:rows] + value[rows:]


def main_kernel(
    parts, count, kr, bs, classes, cp, nodes,
    req_ref, cols_ref, colv_ref, tiles_hbm, feat_ref, lab_ref, w1_ref, w2t_ref,
    logits_ref, sums_ref,
    idx_out, idx_in, stage, feat_tab, agg_tab, tiles, chain, adj,
    part_two, in_two, sum_two, part_one, in_one, sum_one, terms, w1t, w2pad, w2t, w2, acc, g_hl, two_acc, one_acc,
    plan_v, plan_s, plan_sem, tile_sem, send_sem, idx_sem, feat_sem, agg_sem,
    rs_two, ag_two, rs_one, ag_one, out_rs_two, out_ag_two, out_rs_one, out_ag_one,
):
    grp = lax.axis_index("grp")
    me = lax.axis_index("dom")
    chips = parts // 2
    my_chip = me // 2
    own_pairs = count // 2
    wide = -(-(count + parts) // 128)
    table = count + parts
    own = count * bs
    hidden = w1_ref.shape[1]
    halves = hidden // 128
    used = halves * cp + hidden

    def partner(place, t, n):
        if n & (n - 1):
            return lax.rem(place + t, n)
        out, bit = place, 1
        while bit < n:
            out += bit * lax.rem(lax.div(t, bit), 2) * (1 - 2 * lax.rem(lax.div(place, bit), 2))
            bit *= 2
        return out

    def send(src, dst, sem, peer, out_sem=send_sem):
        return pltpu.make_async_remote_copy(
            src_ref=src, dst_ref=dst, send_sem=out_sem.at[peer], recv_sem=sem.at[me],
            device_id=(grp, peer), device_id_type=pl.DeviceIdType.MESH,
        )

    def arrival(buffer, sem, peer):
        return pltpu.make_async_remote_copy(
            src_ref=buffer, dst_ref=buffer, send_sem=send_sem.at[peer], recv_sem=sem.at[peer],
            device_id=(grp, peer), device_id_type=pl.DeviceIdType.MESH,
        )

    def each_peer(body):
        def step(s, _):
            body(partner(me, parts - s, parts))
            return 0

        lax.fori_loop(1, parts, step, 0)

    def tile_copy(row):
        return pltpu.make_async_copy(tiles_hbm.at[row], tiles.at[row], tile_sem.at[row])

    for row in range(count):
        tile_copy(row).start()

    barrier = pltpu.get_barrier_semaphore()
    each_peer(lambda peer: pl.semaphore_signal(
        barrier, inc=1, device_id=(grp, peer), device_id_type=pl.DeviceIdType.MESH))
    w1t[...] = w1_ref[...].astype(F32).T.astype(BF16)
    w2pad[...] = jnp.zeros(w2pad.shape, F32)
    w2pad[0:classes, :] = w2t_ref[...].astype(F32)
    w2t[...] = w2pad[0:cp, :].astype(BF16)
    w2[...] = w2pad[...].T[:, 0:cp].astype(BF16)
    for b in range(count):
        feat_tab[b] = feat_ref[b * bs:(b + 1) * bs, :]
    slot = lax.broadcasted_iota(jnp.int32, (1, kr), 1)
    lane = lax.broadcasted_iota(jnp.int32, (1, 128), 1)
    plan_v[...] = jnp.zeros(plan_v.shape, jnp.int32)

    def plan_tile(k, held):
        out = []
        for row in range(count):
            col = cols_ref[row, k]
            prev, lasts = held[row][0], held[row][1:]
            same = jnp.logical_and(colv_ref[row:row + 1, :] == col, slot > k)
            new = [jnp.where(same, k + 1, prev)]
            for w in range(wide):
                new.append(jnp.where(lane + 128 * w == col, k + 1, lasts[w]))
            out.append(tuple(new))
        return tuple(out)

    none = (jnp.zeros((1, kr), jnp.int32),) + (jnp.zeros((1, 128), jnp.int32),) * wide
    plans = lax.fori_loop(0, kr, plan_tile, (none,) * count, unroll=4)
    for row in range(count):
        plan_v[row:row + 1, 0:kr] = plans[row][0]
        for w in range(wide):
            at = 8 * (1 + w) + row
            plan_v[at:at + 1, :] = plans[row][1 + w]
    plan_copy = pltpu.make_async_copy(plan_v, plan_s, plan_sem)
    plan_copy.start()
    plan_copy.wait()
    pl.semaphore_wait(barrier, parts - 1)

    def ask(peer):
        idx_out[peer] = jnp.full((8, 128), req_ref[0, peer], jnp.int32)
        send(idx_out.at[peer], idx_in.at[me], idx_sem, peer).start()

    each_peer(ask)
    idx_in[me] = jnp.full((8, 128), req_ref[0, me], jnp.int32)
    each_peer(lambda peer: send(idx_out.at[peer], idx_in.at[me], idx_sem, peer).wait_send())

    def pick(peer, tab):
        wanted = jnp.broadcast_to(idx_in[peer][:1], tab.shape[1:])
        out = tab[0].astype(F32)
        for b in range(1, count):
            out = jnp.where(wanted == b, tab[b].astype(F32), out)
        return out.astype(BF16)

    def exchange(tab, sem, first):
        def go(peer):
            if first:
                arrival(idx_in.at[peer], idx_sem, peer).wait_recv()
            stage[peer] = pick(peer, tab)
            send(stage.at[peer], tab.at[count + me], sem, peer).start()

        each_peer(go)
        tab[count + me] = pick(me, tab)

    def sent(tab, sem):
        each_peer(lambda peer: send(stage.at[peer], tab.at[count + me], sem, peer).wait_send())

    exchange(feat_tab, feat_sem, True)

    chain[0] = jnp.zeros((bs, bs), F32)

    def merge_row(row, _):
        tile_copy(row).wait()

        def add(k, _):
            chain[k + 1] = tiles[row, k].astype(F32) + chain[plan_s[row, k]]
            return 0

        lax.fori_loop(0, kr, add, 0, unroll=4)
        rows = pl.ds(pl.multiple_of(row * bs, bs), bs)

        def put(c, _):
            last = plan_s[8 * (1 + lax.div(c, 128)) + row, lax.rem(c, 128)]
            adj[rows, pl.ds(pl.multiple_of(c * bs, bs), bs)] = chain[last].astype(BF16)
            return 0

        lax.fori_loop(0, table, put, 0, unroll=2)
        return 0

    lax.fori_loop(0, count, merge_row, 0)

    each_peer(lambda peer: arrival(feat_tab.at[count + peer], feat_sem, peer).wait_recv())

    def aggregate_row(row, _):
        total = jnp.zeros((bs, feat_ref.shape[1]), F32)
        for k in range(0, kr, 2):
            pair = jnp.concatenate(
                [feat_tab[cols_ref[row, k]], feat_tab[cols_ref[row, k + 1]]], axis=0)
            total += dot(jnp.concatenate([tiles[row, k], tiles[row, k + 1]], axis=1), pair)
        agg_tab[row] = total.astype(BF16)
        return 0

    lax.fori_loop(0, count, aggregate_row, 0)
    sent(feat_tab, feat_sem)

    exchange(agg_tab, agg_sem, False)

    def pair_cols(j):
        return adj[:, pl.ds(pl.multiple_of(j * 2 * bs, 2 * bs), 2 * bs)]

    def pair_agg(j):
        return agg_tab[pl.ds(2 * j, 2)].reshape(2 * bs, w1_ref.shape[0])

    def forward(j):
        pre = dot_nt(w1t[...], pair_agg(j))
        prod = dot(w2t[...], jnp.maximum(pre, 0.0).astype(BF16))
        return fold_rows(dot_nt(split_rows(prod), pair_cols(j)), cp)

    acc[...] = forward(0)
    for j in range(1, own_pairs):
        acc[...] += forward(j)

    def halo(s, _):
        chip = partner(my_chip, s, chips)
        for core in range(2):
            peer = 2 * chip + core

            @pl.when(peer != me)
            def _():
                arrival(agg_tab.at[count + peer], agg_sem, peer).wait_recv()

        acc[...] += forward(own_pairs + chip)
        return 0

    lax.fori_loop(0, chips, halo, 0)
    sent(agg_tab, agg_sem)

    logits = acc[...]
    logits_ref[...] = logits
    rows = lax.broadcasted_iota(jnp.int32, (cp, own), 0)
    real = rows < classes
    top = jnp.max(jnp.where(real, logits, -jnp.inf), axis=0, keepdims=True)
    expo = jnp.where(real, jnp.exp(logits - top), 0.0)
    probs = expo / jnp.sum(expo, axis=0, keepdims=True)
    labels = jnp.concatenate([lab_ref[b:b + 1, :] for b in range(count)], axis=1)
    onehot = jnp.where(rows == labels, 1.0, 0.0)
    g_hl[...] = split_rows((probs - onehot) / math.sqrt(nodes))

    two_acc[...] = jnp.zeros(two_acc.shape, F32)
    one_acc[...] = jnp.zeros(one_acc.shape, F32)

    def backward_two(j):
        pre = dot_nt(w1t[...], pair_agg(j))
        term = split_rows(fold_rows(dot(g_hl[...], pair_cols(j)), cp))
        two_acc[...] += fold_rows(dot_nt(term, jnp.maximum(pre, 0.0).astype(BF16)), cp)
        return term

    def backward_one(j, term):
        agg = pair_agg(j)
        pre = dot_nt(w1t[...], agg)
        grad_hidden = dot(w2[...], term[:cp]) + dot(w2[...], term[cp:])
        grad_pre = jnp.where(pre > 0.0, grad_hidden, 0.0)
        one_acc[...] += fold_rows(dot(split_rows(grad_pre), agg), hidden)

    def share(rows, peer):
        return pl.ds(pl.multiple_of(peer * rows, 16), rows)

    def scatter(grads, inbox, sem, out_sem):
        rows = inbox.shape[1]
        each_peer(lambda peer: send(
            grads.at[share(rows, peer)], inbox.at[me], sem, peer, out_sem).start())
        inbox[me] = grads[share(rows, me)]

    def collect(grads, inbox, final, sem, out_sem):
        rows = inbox.shape[1]
        each_peer(lambda peer: arrival(inbox.at[peer], sem, peer).wait_recv())
        total = lax.fori_loop(
            0, parts, lambda p, t: t + inbox[p].astype(F32), jnp.zeros((rows, 128), F32))
        final[share(rows, me)] = total.astype(BF16)
        each_peer(lambda peer: send(
            grads.at[share(rows, peer)], inbox.at[me], sem, peer, out_sem).wait_send())

    def hand_round(final, rows, sem, out_sem):
        each_peer(lambda peer: send(
            final.at[share(rows, me)], final.at[share(rows, me)], sem, peer, out_sem).start())

    def gather(final, rows, sem, out_sem):
        each_peer(lambda peer: arrival(final.at[share(rows, peer)], sem, peer).wait_recv())
        each_peer(lambda peer: send(
            final.at[share(rows, me)], final.at[share(rows, me)], sem, peer, out_sem).wait_send())

    rows_two, rows_one = in_two.shape[1], in_one.shape[1]
    pairs = table // 2
    keep = terms.shape[0] == pairs

    def first_pass(j, _):
        term = backward_two(j)
        if keep:
            terms[j] = term
        else:
            backward_one(j, term)
        return 0

    lax.fori_loop(0, pairs, first_pass, 0, unroll=keep)
    for h in range(halves):
        part_two[h * cp:(h + 1) * cp, :] = two_acc[:, h * 128:(h + 1) * 128].astype(BF16)
    if halves * cp < parts * rows_two:
        part_two[halves * cp:, :] = jnp.zeros((parts * rows_two - halves * cp, 128), BF16)
    scatter(part_two, in_two, rs_two, out_rs_two)

    if keep:
        def second_pass(j, _):
            backward_one(j, terms[j])
            return 0

        lax.fori_loop(0, pairs, second_pass, 0, unroll=True)
    part_one[0:hidden, :] = one_acc[...].astype(BF16)
    if hidden < parts * rows_one:
        part_one[hidden:, :] = jnp.zeros((parts * rows_one - hidden, 128), BF16)
    scatter(part_one, in_one, rs_one, out_rs_one)

    collect(part_two, in_two, sum_two, rs_two, out_rs_two)
    hand_round(sum_two, rows_two, ag_two, out_ag_two)
    collect(part_one, in_one, sum_one, rs_one, out_rs_one)
    hand_round(sum_one, rows_one, ag_one, out_ag_one)
    gather(sum_two, rows_two, ag_two, out_ag_two)
    sums_ref[0:halves * cp, :] = sum_two[0:halves * cp, :].astype(F32)
    gather(sum_one, rows_one, ag_one, out_ag_one)
    sums_ref[halves * cp:used, :] = sum_one[0:hidden, :].astype(F32)


def place_kernel(classes, cp, hidden, logits_ref, sums_ref, out_ref, one_ref, two_ref):
    halves = hidden // 128
    out_ref[...] = logits_ref[0:classes, :]
    for h in range(halves):
        two_ref[:, h * 128:(h + 1) * 128] = sums_ref[h * cp:h * cp + classes, :]
    one_ref[...] = sums_ref[halves * cp:, :].T


def local(features, block_tiles, block_cols, halo_request, labels, weight_one, weight_two):
    parts = lax.axis_size("dom")
    count, bs, kr, _ = block_tiles.shape
    width = features.shape[1]
    hidden, classes = weight_two.shape
    cp = -(-classes // 16) * 16
    cw = -(-classes // 128) * 128
    own = count * bs
    table = count + parts
    used = (hidden // 128) * cp + hidden
    rows_two = -(-((hidden // 128) * cp) // (16 * parts)) * 16
    rows_one = -(-hidden // (16 * parts)) * 16
    tiles = block_tiles.transpose(0, 2, 1, 3)
    plan = (8 * (1 + -(-table // 128)), 128)
    vmem = pl.BlockSpec(memory_space=pltpu.VMEM)
    smem = pl.BlockSpec(memory_space=pltpu.SMEM)
    dma = pltpu.SemaphoreType.DMA((parts,))
    logits, sums = pl.pallas_call(
        functools.partial(main_kernel, parts, count, kr, bs, classes, cp, parts * own),
        out_shape=(
            jax.ShapeDtypeStruct((cp, own), F32),
            jax.ShapeDtypeStruct((used, 128), F32),
        ),
        in_specs=[smem, smem, vmem, pl.BlockSpec(memory_space=pl.ANY)] + [vmem] * 4,
        out_specs=(vmem, vmem),
        scratch_shapes=[
            pltpu.VMEM((parts, 8, 128), jnp.int32),
            pltpu.VMEM((parts, 8, 128), jnp.int32),
            pltpu.VMEM((parts, bs, width), BF16),
            pltpu.VMEM((table, bs, width), BF16),
            pltpu.VMEM((table, bs, width), BF16),
            pltpu.VMEM((count, kr, bs, bs), BF16),
            pltpu.VMEM((kr + 1, bs, bs), F32),
            pltpu.VMEM((own, table * bs), BF16),
            pltpu.VMEM((parts * rows_two, 128), BF16),
            pltpu.VMEM((parts, rows_two, 128), BF16),
            pltpu.VMEM((parts * rows_two, 128), BF16),
            pltpu.VMEM((parts * rows_one, 128), BF16),
            pltpu.VMEM((parts, rows_one, 128), BF16),
            pltpu.VMEM((parts * rows_one, 128), BF16),
            pltpu.VMEM((table // 2 if table <= 32 else 1, 2 * cp, 2 * bs), BF16),
            pltpu.VMEM((hidden, width), BF16),
            pltpu.VMEM((cw, hidden), F32),
            pltpu.VMEM((cp, hidden), BF16),
            pltpu.VMEM((hidden, cp), BF16),
            pltpu.VMEM((cp, own), F32),
            pltpu.VMEM((2 * cp, own), BF16),
            pltpu.VMEM((cp, hidden), F32),
            pltpu.VMEM((hidden, width), F32),
            pltpu.VMEM(plan, jnp.int32),
            pltpu.SMEM(plan, jnp.int32),
            pltpu.SemaphoreType.DMA,
            pltpu.SemaphoreType.DMA((count,)),
            dma, dma, dma, dma,
            dma, dma, dma, dma, dma, dma, dma, dma,
        ],
        compiler_params=pltpu.CompilerParams(
            collective_id=0, has_side_effects=True, vmem_limit_bytes=62 * 1024 * 1024),
        name="graph_layers",
    )(halo_request, block_cols, block_cols, tiles, features, labels.reshape(count, bs),
      weight_one, weight_two.T)
    logits, one, two = pl.pallas_call(
        functools.partial(place_kernel, classes, cp, hidden),
        out_shape=(
            jax.ShapeDtypeStruct((classes, own), F32),
            jax.ShapeDtypeStruct((width, hidden), F32),
            jax.ShapeDtypeStruct((classes, hidden), F32),
        ),
        in_specs=[vmem, vmem],
        out_specs=(vmem, vmem, vmem),
        name="place_results",
    )(logits, sums)
    return (logits.T, one, two.T)


def solution(mesh):
    placed = (
        P(("grp", "dom"), None),
        P(("grp", "dom"), None, None, None),
        P(("grp", "dom"), None),
        P(("grp", "dom"), None),
        P(("grp", "dom")),
        P(),
        P(),
    )
    return jax.shard_map(
        local,
        mesh=mesh,
        in_specs=placed,
        out_specs=(P(("grp", "dom"), None), P("grp", None), P("grp", None)),
        check_vma=False,
    )
```

```python
import functools
import math

import jax
import jax.numpy as jnp
from jax import lax
from jax.experimental import pallas as pl
from jax.experimental.pallas import tpu as pltpu
from jax.sharding import PartitionSpec as P

F32 = jnp.float32
BF16 = jnp.bfloat16
NT = (((1,), (1,)), ((), ()))


def dot(left, right):
    return jnp.dot(left, right, preferred_element_type=F32)


def dot_nt(left, right):
    return lax.dot_general(left, right, NT, preferred_element_type=F32)


def split_rows(value):
    high = value.astype(BF16)
    low = (value - high.astype(F32)).astype(BF16)
    return jnp.concatenate([high, low], axis=0)


def fold_rows(value, rows):
    return value[:rows] + value[rows:]


def main_kernel(
    parts, count, kr, bs, classes, cp, nodes,
    req_ref, cols_ref, colv_ref, tiles_hbm, feat_ref, lab_ref, w1_ref, w2t_ref,
    logits_ref, sums_ref,
    idx_out, idx_in, stage, feat_tab, agg_tab, tiles, chain, adj,
    part_two, in_two, sum_two, part_one, in_one, sum_one, terms, w1t, w2pad, w2t, w2, acc, g_hl, two_acc, one_acc,
    plan_v, plan_s, plan_sem, tile_sem, send_sem, idx_sem, feat_sem, agg_sem,
    rs_two, ag_two, rs_one, ag_one, out_rs_two, out_ag_two, out_rs_one, out_ag_one,
):
    grp = lax.axis_index("grp")
    me = lax.axis_index("dom")
    chips = parts // 2
    my_chip = me // 2
    own_pairs = count // 2
    wide = -(-(count + parts) // 128)
    table = count + parts
    own = count * bs
    hidden = w1_ref.shape[1]
    halves = hidden // 128
    used = halves * cp + hidden

    def flips(place, n):
        bits = [1 << b for b in range(n.bit_length() - 1)]
        return [(bit, bit - 2 * bit * lax.rem(lax.div(place, bit), 2)) for bit in bits]

    my_flips, chip_flips = flips(me, parts), flips(my_chip, chips)

    def partner(place, place_flips, t, n):
        if n & (n - 1):
            return lax.rem(place + t, n)
        out = place
        for bit, change in place_flips:
            if isinstance(t, int):
                out = out + change if t & bit else out
            else:
                out += lax.rem(lax.div(t, bit), 2) * change
        return out

    def each_far(body, unroll=parts <= 16):
        def step(s, _):
            body(partner(me, my_flips, parts - s, parts))
            return 0

        if unroll:
            for s in range(1, parts):
                step(s, 0)
        else:
            lax.fori_loop(1, parts, step, 0)

    def send(src, dst, sem, peer, out_sem=send_sem):
        return pltpu.make_async_remote_copy(
            src_ref=src, dst_ref=dst, send_sem=out_sem.at[peer], recv_sem=sem.at[me],
            device_id=(grp, peer), device_id_type=pl.DeviceIdType.MESH,
        )

    def arrival(buffer, sem, peer):
        return pltpu.make_async_remote_copy(
            src_ref=buffer, dst_ref=buffer, send_sem=send_sem.at[peer], recv_sem=sem.at[peer],
            device_id=(grp, peer), device_id_type=pl.DeviceIdType.MESH,
        )

    def each_peer(body):
        def step(s, _):
            body(lax.rem(me + s, parts))
            return 0

        lax.fori_loop(1, parts, step, 0)

    def tile_copy(row):
        return pltpu.make_async_copy(tiles_hbm.at[row], tiles.at[row], tile_sem.at[row])

    for row in range(count):
        tile_copy(row).start()

    barrier = pltpu.get_barrier_semaphore()
    each_peer(lambda peer: pl.semaphore_signal(
        barrier, inc=1, device_id=(grp, peer), device_id_type=pl.DeviceIdType.MESH))
    w1t[...] = w1_ref[...].astype(F32).T.astype(BF16)
    w2pad[...] = jnp.zeros(w2pad.shape, F32)
    w2pad[0:classes, :] = w2t_ref[...].astype(F32)
    w2t[...] = w2pad[0:cp, :].astype(BF16)
    w2[...] = w2pad[...].T[:, 0:cp].astype(BF16)
    for b in range(count):
        feat_tab[b] = feat_ref[b * bs:(b + 1) * bs, :]
    slot = lax.broadcasted_iota(jnp.int32, (1, kr), 1)
    lane = lax.broadcasted_iota(jnp.int32, (1, 128), 1)
    plan_v[...] = jnp.zeros(plan_v.shape, jnp.int32)

    def plan_tile(k, held):
        out = []
        for row in range(count):
            col = cols_ref[row, k]
            prev, lasts = held[row][0], held[row][1:]
            same = jnp.logical_and(colv_ref[row:row + 1, :] == col, slot > k)
            new = [jnp.where(same, k + 1, prev)]
            for w in range(wide):
                new.append(jnp.where(lane + 128 * w == col, k + 1, lasts[w]))
            out.append(tuple(new))
        return tuple(out)

    none = (jnp.zeros((1, kr), jnp.int32),) + (jnp.zeros((1, 128), jnp.int32),) * wide
    plans = lax.fori_loop(0, kr, plan_tile, (none,) * count, unroll=4)
    for row in range(count):
        plan_v[row:row + 1, 0:kr] = plans[row][0]
        for w in range(wide):
            at = 8 * (1 + w) + row
            plan_v[at:at + 1, :] = plans[row][1 + w]
    plan_copy = pltpu.make_async_copy(plan_v, plan_s, plan_sem)
    plan_copy.start()
    plan_copy.wait()
    pl.semaphore_wait(barrier, parts - 1)

    def ask(peer):
        idx_out[peer] = jnp.full((8, 128), req_ref[0, peer], jnp.int32)
        send(idx_out.at[peer], idx_in.at[me], idx_sem, peer).start()

    each_far(ask)
    idx_in[me] = jnp.full((8, 128), req_ref[0, me], jnp.int32)
    each_peer(lambda peer: send(idx_out.at[peer], idx_in.at[me], idx_sem, peer).wait_send())

    def pick(peer, tab):
        wanted = jnp.broadcast_to(idx_in[peer][:1], tab.shape[1:])
        out = tab[0].astype(F32)
        for b in range(1, count):
            out = jnp.where(wanted == b, tab[b].astype(F32), out)
        return out.astype(BF16)

    def exchange(tab, sem, first):
        def go(peer):
            if first:
                arrival(idx_in.at[peer], idx_sem, peer).wait_recv()
            stage[peer] = pick(peer, tab)
            send(stage.at[peer], tab.at[count + me], sem, peer).start()

        each_far(go, False)
        tab[count + me] = pick(me, tab)

    def sent(tab, sem):
        each_peer(lambda peer: send(stage.at[peer], tab.at[count + me], sem, peer).wait_send())

    exchange(feat_tab, feat_sem, True)

    chain[0] = jnp.zeros((bs, bs), F32)

    def merge_row(row, _):
        tile_copy(row).wait()

        def add(k, _):
            chain[k + 1] = tiles[row, k].astype(F32) + chain[plan_s[row, k]]
            return 0

        lax.fori_loop(0, kr, add, 0, unroll=4)
        rows = pl.ds(pl.multiple_of(row * bs, bs), bs)

        def put(c, _):
            last = plan_s[8 * (1 + lax.div(c, 128)) + row, lax.rem(c, 128)]
            adj[rows, pl.ds(pl.multiple_of(c * bs, bs), bs)] = chain[last].astype(BF16)
            return 0

        lax.fori_loop(0, table, put, 0, unroll=2)
        return 0

    lax.fori_loop(0, count, merge_row, 0)

    each_peer(lambda peer: arrival(feat_tab.at[count + peer], feat_sem, peer).wait_recv())

    def aggregate_row(row, _):
        total = jnp.zeros((bs, feat_ref.shape[1]), F32)
        for k in range(0, kr, 2):
            pair = jnp.concatenate(
                [feat_tab[cols_ref[row, k]], feat_tab[cols_ref[row, k + 1]]], axis=0)
            total += dot(jnp.concatenate([tiles[row, k], tiles[row, k + 1]], axis=1), pair)
        agg_tab[row] = total.astype(BF16)
        return 0

    lax.fori_loop(0, count, aggregate_row, 0)
    sent(feat_tab, feat_sem)

    exchange(agg_tab, agg_sem, False)

    def pair_cols(j):
        return adj[:, pl.ds(pl.multiple_of(j * 2 * bs, 2 * bs), 2 * bs)]

    def pair_agg(j):
        return agg_tab[pl.ds(2 * j, 2)].reshape(2 * bs, w1_ref.shape[0])

    def forward(j):
        pre = dot_nt(w1t[...], pair_agg(j))
        prod = dot(w2t[...], jnp.maximum(pre, 0.0).astype(BF16))
        return fold_rows(dot_nt(split_rows(prod), pair_cols(j)), cp)

    acc[...] = forward(0)
    for j in range(1, own_pairs):
        acc[...] += forward(j)

    def halo(s, _):
        chip = partner(my_chip, chip_flips, s, chips)
        for core in range(2):
            peer = 2 * chip + core

            @pl.when(peer != me)
            def _():
                arrival(agg_tab.at[count + peer], agg_sem, peer).wait_recv()

        acc[...] += forward(own_pairs + chip)
        return 0

    lax.fori_loop(0, chips, halo, 0)
    sent(agg_tab, agg_sem)

    logits = acc[...]
    logits_ref[...] = logits
    rows = lax.broadcasted_iota(jnp.int32, (cp, own), 0)
    real = rows < classes
    top = jnp.max(jnp.where(real, logits, -jnp.inf), axis=0, keepdims=True)
    expo = jnp.where(real, jnp.exp(logits - top), 0.0)
    probs = expo / jnp.sum(expo, axis=0, keepdims=True)
    labels = jnp.concatenate([lab_ref[b:b + 1, :] for b in range(count)], axis=1)
    onehot = jnp.where(rows == labels, 1.0, 0.0)
    g_hl[...] = split_rows((probs - onehot) / math.sqrt(nodes))

    two_acc[...] = jnp.zeros(two_acc.shape, F32)
    one_acc[...] = jnp.zeros(one_acc.shape, F32)

    def backward_two(j):
        pre = dot_nt(w1t[...], pair_agg(j))
        term = split_rows(fold_rows(dot(g_hl[...], pair_cols(j)), cp))
        two_acc[...] += fold_rows(dot_nt(term, jnp.maximum(pre, 0.0).astype(BF16)), cp)
        return term

    def backward_one(j, term):
        agg = pair_agg(j)
        pre = dot_nt(w1t[...], agg)
        grad_hidden = dot(w2[...], term[:cp]) + dot(w2[...], term[cp:])
        grad_pre = jnp.where(pre > 0.0, grad_hidden, 0.0)
        one_acc[...] += fold_rows(dot(split_rows(grad_pre), agg), hidden)

    def share(rows, peer):
        return pl.ds(pl.multiple_of(peer * rows, 16), rows)

    def scatter(grads, inbox, sem, out_sem):
        rows = inbox.shape[1]
        each_far(lambda peer: send(
            grads.at[share(rows, peer)], inbox.at[me], sem, peer, out_sem).start())
        inbox[me] = grads[share(rows, me)]

    def collect(grads, inbox, final, sem, out_sem):
        rows = inbox.shape[1]
        each_peer(lambda peer: arrival(inbox.at[peer], sem, peer).wait_recv())
        total = lax.fori_loop(
            0, parts, lambda p, t: t + inbox[p].astype(F32), jnp.zeros((rows, 128), F32))
        final[share(rows, me)] = total.astype(BF16)
        each_peer(lambda peer: send(
            grads.at[share(rows, peer)], inbox.at[me], sem, peer, out_sem).wait_send())

    def hand_round(final, rows, sem, out_sem):
        each_far(lambda peer: send(
            final.at[share(rows, me)], final.at[share(rows, me)], sem, peer, out_sem).start())

    def gather(final, rows, sem, out_sem):
        each_peer(lambda peer: arrival(final.at[share(rows, peer)], sem, peer).wait_recv())
        each_peer(lambda peer: send(
            final.at[share(rows, me)], final.at[share(rows, me)], sem, peer, out_sem).wait_send())

    rows_two, rows_one = in_two.shape[1], in_one.shape[1]
    pairs = table // 2
    keep = terms.shape[0] == pairs

    def first_pass(j, _):
        term = backward_two(j)
        if keep:
            terms[j] = term
        else:
            backward_one(j, term)
        return 0

    lax.fori_loop(0, pairs, first_pass, 0, unroll=keep)
    for h in range(halves):
        part_two[h * cp:(h + 1) * cp, :] = two_acc[:, h * 128:(h + 1) * 128].astype(BF16)
    if halves * cp < parts * rows_two:
        part_two[halves * cp:, :] = jnp.zeros((parts * rows_two - halves * cp, 128), BF16)
    scatter(part_two, in_two, rs_two, out_rs_two)

    if keep:
        def second_pass(j, _):
            backward_one(j, terms[j])
            return 0

        lax.fori_loop(0, pairs, second_pass, 0, unroll=True)
    part_one[0:hidden, :] = one_acc[...].astype(BF16)
    if hidden < parts * rows_one:
        part_one[hidden:, :] = jnp.zeros((parts * rows_one - hidden, 128), BF16)
    scatter(part_one, in_one, rs_one, out_rs_one)

    collect(part_two, in_two, sum_two, rs_two, out_rs_two)
    hand_round(sum_two, rows_two, ag_two, out_ag_two)
    collect(part_one, in_one, sum_one, rs_one, out_rs_one)
    hand_round(sum_one, rows_one, ag_one, out_ag_one)
    gather(sum_two, rows_two, ag_two, out_ag_two)
    sums_ref[0:halves * cp, :] = sum_two[0:halves * cp, :].astype(F32)
    gather(sum_one, rows_one, ag_one, out_ag_one)
    sums_ref[halves * cp:used, :] = sum_one[0:hidden, :].astype(F32)


def place_kernel(classes, cp, hidden, logits_ref, sums_ref, out_ref, one_ref, two_ref):
    halves = hidden // 128
    out_ref[...] = logits_ref[0:classes, :]
    for h in range(halves):
        two_ref[:, h * 128:(h + 1) * 128] = sums_ref[h * cp:h * cp + classes, :]
    one_ref[...] = sums_ref[halves * cp:, :].T


def local(features, block_tiles, block_cols, halo_request, labels, weight_one, weight_two):
    parts = lax.axis_size("dom")
    count, bs, kr, _ = block_tiles.shape
    width = features.shape[1]
    hidden, classes = weight_two.shape
    cp = -(-classes // 16) * 16
    cw = -(-classes // 128) * 128
    own = count * bs
    table = count + parts
    used = (hidden // 128) * cp + hidden
    rows_two = -(-((hidden // 128) * cp) // (16 * parts)) * 16
    rows_one = -(-hidden // (16 * parts)) * 16
    tiles = block_tiles.transpose(0, 2, 1, 3)
    plan = (8 * (1 + -(-table // 128)), 128)
    vmem = pl.BlockSpec(memory_space=pltpu.VMEM)
    smem = pl.BlockSpec(memory_space=pltpu.SMEM)
    dma = pltpu.SemaphoreType.DMA((parts,))
    logits, sums = pl.pallas_call(
        functools.partial(main_kernel, parts, count, kr, bs, classes, cp, parts * own),
        out_shape=(
            jax.ShapeDtypeStruct((cp, own), F32),
            jax.ShapeDtypeStruct((used, 128), F32),
        ),
        in_specs=[smem, smem, vmem, pl.BlockSpec(memory_space=pl.ANY)] + [vmem] * 4,
        out_specs=(vmem, vmem),
        scratch_shapes=[
            pltpu.VMEM((parts, 8, 128), jnp.int32),
            pltpu.VMEM((parts, 8, 128), jnp.int32),
            pltpu.VMEM((parts, bs, width), BF16),
            pltpu.VMEM((table, bs, width), BF16),
            pltpu.VMEM((table, bs, width), BF16),
            pltpu.VMEM((count, kr, bs, bs), BF16),
            pltpu.VMEM((kr + 1, bs, bs), F32),
            pltpu.VMEM((own, table * bs), BF16),
            pltpu.VMEM((parts * rows_two, 128), BF16),
            pltpu.VMEM((parts, rows_two, 128), BF16),
            pltpu.VMEM((parts * rows_two, 128), BF16),
            pltpu.VMEM((parts * rows_one, 128), BF16),
            pltpu.VMEM((parts, rows_one, 128), BF16),
            pltpu.VMEM((parts * rows_one, 128), BF16),
            pltpu.VMEM((table // 2 if table <= 32 else 1, 2 * cp, 2 * bs), BF16),
            pltpu.VMEM((hidden, width), BF16),
            pltpu.VMEM((cw, hidden), F32),
            pltpu.VMEM((cp, hidden), BF16),
            pltpu.VMEM((hidden, cp), BF16),
            pltpu.VMEM((cp, own), F32),
            pltpu.VMEM((2 * cp, own), BF16),
            pltpu.VMEM((cp, hidden), F32),
            pltpu.VMEM((hidden, width), F32),
            pltpu.VMEM(plan, jnp.int32),
            pltpu.SMEM(plan, jnp.int32),
            pltpu.SemaphoreType.DMA,
            pltpu.SemaphoreType.DMA((count,)),
            dma, dma, dma, dma,
            dma, dma, dma, dma, dma, dma, dma, dma,
        ],
        compiler_params=pltpu.CompilerParams(
            collective_id=0, has_side_effects=True, vmem_limit_bytes=62 * 1024 * 1024),
        name="graph_layers",
    )(halo_request, block_cols, block_cols, tiles, features, labels.reshape(count, bs),
      weight_one, weight_two.T)
    logits, one, two = pl.pallas_call(
        functools.partial(place_kernel, classes, cp, hidden),
        out_shape=(
            jax.ShapeDtypeStruct((classes, own), F32),
            jax.ShapeDtypeStruct((width, hidden), F32),
            jax.ShapeDtypeStruct((classes, hidden), F32),
        ),
        in_specs=[vmem, vmem],
        out_specs=(vmem, vmem, vmem),
        name="place_results",
    )(logits, sums)
    return (logits.T, one, two.T)


def solution(mesh):
    placed = (
        P(("grp", "dom"), None),
        P(("grp", "dom"), None, None, None),
        P(("grp", "dom"), None),
        P(("grp", "dom"), None),
        P(("grp", "dom")),
        P(),
        P(),
    )
    return jax.shard_map(
        local,
        mesh=mesh,
        in_specs=placed,
        out_specs=(P(("grp", "dom"), None), P("grp", None), P("grp", None)),
        check_vma=False,
    )
```
